32 devices in a mesh: groups: 2 (over x), docs: 8 (over z, y), layers: 2 (over core).
Axes of the slice: x: 2, y: 2, z: 4, core: 2. Of those that a mesh axis runs over, the one named last changes fastest.
Arguments:
- doc_grads: bfloat16 [12288, 4, 4096], P(('groups', 'docs'), 'layers'), parts along dimension 0, may hold values from -6 to 6
- query_grads: bfloat16 [512, 4, 4096], P(('groups', 'docs'), 'layers'), parts along dimension 0, may hold values from -0.046875 to 0.046875
- doc_lengths: int32 [12288], P(('groups', 'docs')), parts along dimension 0, may hold values from 1 to 16
Outputs:
- scores: float32 [12288, 256], P(('groups', 'docs'), 'layers'), parts along dimension 0
The draws below stay inside these ranges and needn't reach their ends.
There are 2 independent parts, one for each index of `groups`. The reference program is written for one: setup_inputs(seed, part) draws one part's arguments, and reference() takes and returns one part's arrays. A program takes and returns all parts, laid end to end along the dimension named above; each array names one. Nothing has to cross between parts.
All inputs are finite; a program needn't handle non-finite values.
Results may differ from the reference program's by a relative error of at most 0.0003.
Values may be sent and summed in bfloat16 or wider, within the bound.
A program may use at most 64 MiB of HBM per device.

```python
import jax
import jax.numpy as jnp

P_SIZE = 4096
QUERIES = 256
LAYERS = 4
DOCS = 6144


def set_ends(drawn, rng, least, high):
    longest = drawn.shape.index(max(drawn.shape))
    spots = []
    for shift in (0, 1):
        where = [jax.random.randint(jax.random.fold_in(rng, axis), (), 0, length) for axis, length in enumerate(drawn.shape)]
        where[longest] = (where[longest] + shift) % drawn.shape[longest]
        spots.append(tuple(where))
    return drawn.at[spots[0]].set(least).at[spots[1]].set(high)


def level_of(key, dims, split, low, high):
    factor_of = 1.0
    for dim, parts in split:
        heights = jax.random.uniform(jax.random.fold_in(jax.random.fold_in(key, 6), dim), (parts,), jnp.float32, low / len(split), high / len(split))
        factor_of = factor_of * jnp.repeat(jnp.exp(heights), dims[dim] // parts).reshape((-1,) + (1,) * (len(dims) - 1 - dim))
    return factor_of


def normal_values(rng, extent, deviation, most, split=(), held_as=jnp.bfloat16):
    entries = jax.random.normal(rng, extent, jnp.float32) * deviation
    if len(split) > 0:
        entries = level_of(rng, extent, split, -0.22, 0.18) * entries
    return jnp.clip(entries, min=-most, max=most).astype(held_as)


def setup_inputs(seed: int = 0, part: int = 0) -> dict:
    splits = jax.random.split(jax.random.key(seed), 4)
    part_keys = jax.random.split(jax.random.fold_in(splits[3], part), 4)
    return {
        "doc_grads": normal_values(part_keys[0], (DOCS, LAYERS, P_SIZE), 1.0, 6.0, ((0, 8), (1, 2))),
        "query_grads": normal_values(part_keys[1], (QUERIES, LAYERS, P_SIZE), (LAYERS * P_SIZE) ** -0.5, 0.046875, ((0, 8), (1, 2))),
        "doc_lengths": set_ends(jax.random.randint(part_keys[2], (DOCS,), 1, 17), jax.random.fold_in(part_keys[2], 1), 1, 16).astype(jnp.int32),
    }


def reference(doc_grads, query_grads, doc_lengths):
    total = jnp.zeros((doc_grads.shape[0], query_grads.shape[0]), jnp.float32)
    for layer in range(LAYERS):
        total = total + jnp.dot(doc_grads[:, layer, :], query_grads[:, layer, :].T, preferred_element_type=jnp.float32)
    return total / doc_lengths.astype(jnp.float32)[:, None]
```

```python
import functools

import jax
import jax.numpy as jnp
from jax import lax
from jax.experimental import pallas as pl
from jax.experimental.pallas import tpu as pltpu
from jax.sharding import PartitionSpec as P

LINE = 4
LAST = 640
STEP = 512
LAG = 5


def pieces_of(depth):
    cuts, at = [], 0
    while at < depth - LAST:
        size = min(STEP, depth - LAST - at)
        cuts.append((at, size))
        at += size
    return cuts + [(at, depth - at)]


def kernel(cuts, docs_ref, q_ref, len_ref, out_ref, docs, own_q, held, acc, other, lengths,
           doc_sem, q_sem, send_sem, recv_sem, x_send, x_recv):
    me = lax.axis_index("docs")
    core = lax.axis_index("layers")
    z, y = me // 2, me % 2
    across = z * 2 + (1 - y)
    rows = q_ref.shape[0]
    last = len(cuts) - 1
    n_docs = docs.shape[0]
    half = out_ref.shape[1]

    def q_copy(c):
        at, size = cuts[c]
        cols = pl.ds(at, size)
        return pltpu.make_async_copy(q_ref.at[:, :, cols], own_q.at[:, :, cols], q_sem.at[c])

    def doc_copy(c):
        at, size = cuts[c]
        cols = pl.ds(at, size)
        return pltpu.make_async_copy(docs_ref.at[:, :, cols], docs.at[:, :, cols], doc_sem.at[c])

    first = [0, last] + list(range(1, last))
    for c in first:
        q_copy(c).start()
    for c in range(last + 1):
        doc_copy(c).start()

    barrier = pltpu.get_barrier_semaphore()

    def greet(target):
        pl.semaphore_signal(barrier, inc=1, device_id=target, device_id_type=pl.DeviceIdType.MESH)

    greet({"docs": across})
    greet({"layers": 1 - core})

    @pl.when(z < LINE - 1)
    def _():
        greet({"docs": me + 2})

    @pl.when(z > 0)
    def _():
        greet({"docs": me - 2})

    def take_own(c):
        at, size = cuts[c]
        q_copy(c).wait()
        mine = pl.ds(pl.multiple_of(me * rows, rows), rows)
        for layer in range(2):
            held[layer, mine, pl.ds(at, size)] = own_q[:, layer, pl.ds(at, size)]

    take_own(0)
    take_own(last)

    pl.semaphore_wait(barrier, 2 + (z + LINE - 1) // LINE + (2 * LINE - 2 - z) // LINE)

    def copy(c, src, way):
        at, size = cuts[c]
        block = held.at[:, pl.ds(pl.multiple_of(src * rows, rows), rows), pl.ds(at, size)]
        return pltpu.make_async_remote_copy(
            src_ref=block,
            dst_ref=block,
            send_sem=send_sem.at[way, c, src],
            recv_sem=recv_sem.at[c, src],
            device_id={"docs": (me + 2, me - 2, across)[way]},
            device_id_type=pl.DeviceIdType.MESH,
        )

    def arrived(c, src, start):
        if start:
            copy(c, src, 2).wait_recv()

    def send(c, src, way, start):
        def act():
            if start:
                copy(c, src, way).start()
            else:
                copy(c, src, way).wait_send()

        if way == 0:
            pl.when(z < LINE - 1)(act)
        elif way == 1:
            pl.when(z > 0)(act)
        else:
            act()

    def stage(c, hops, start=True):
        if hops == 0:
            send(c, me, 0, start)
            send(c, me, 1, start)
            if c == last:
                arrived(c, across, start)
                send(c, across, 0, start)
                send(c, across, 1, start)
            else:
                send(c, me, 2, start)
            return
        for lane in (y,) if c < last else (y, 1 - y):

            @pl.when(z >= hops)
            def _():
                src = (z - hops) * 2 + lane
                arrived(c, src, start)
                send(c, src, 0, start)
                if c < last:
                    send(c, src, 2, start)

            @pl.when(z + hops < LINE)
            def _():
                src = (z + hops) * 2 + lane
                arrived(c, src, start)
                send(c, src, 1, start)
                if c < last:
                    send(c, src, 2, start)

    def add(c, at_row, n_rows, first_one):
        at, size = cuts[c]
        these = pl.ds(at_row, n_rows)
        cols = pl.ds(at, size)
        total = None
        for layer in range(2):
            term = lax.dot_general(
                docs[these, layer, cols], held[layer, :, cols], (((1,), (1,)), ((), ())),
                preferred_element_type=jnp.float32,
            )
            total = term if total is None else total + term
        if first_one:
            acc[these, :] = total
        else:
            acc[these, :] += total

    def compute(c):
        doc_copy(c).wait()
        for line in range(LINE):
            arrived(c, line * 2 + (1 - y), True)
        add(c, 0, n_docs, c == 0)

    stage(0, 0)
    send(last, me, 2, True)
    for r in range(n_docs // 128):
        row = len_ref[pl.ds(r, 1), :].astype(jnp.float32)
        lengths[pl.ds(r * 128, 128), :] = jnp.broadcast_to(row, (128, 128)).T
    done = 0
    for step in range(1, last + LINE):
        if step < last:
            take_own(step)
        if step <= last:
            stage(step, 0)
        for hops in range(1, LINE):
            if 0 <= step - hops <= last:
                stage(step - hops, hops)
        if step >= LAG and done < last:
            compute(done)
            done += 1
    while done < last:
        compute(done)
        done += 1

    doc_copy(last).wait()
    blocks = 3
    height = n_docs // blocks

    def swap(b):
        these = pl.ds(b * height, height)
        return pltpu.make_async_remote_copy(
            src_ref=acc.at[these, pl.ds(pl.multiple_of((1 - core) * half, half), half)],
            dst_ref=other.at[these, :],
            send_sem=x_send.at[b],
            recv_sem=x_recv.at[b],
            device_id={"layers": 1 - core},
            device_id_type=pl.DeviceIdType.MESH,
        )

    for b in range(blocks):
        add(last, b * height, height, False)
        swap(b).start()
    for b in range(blocks):
        these = pl.ds(b * height, height)
        swap(b).wait_recv()
        mine = acc[these, pl.ds(pl.multiple_of(core * half, half), half)]
        out_ref[these, :] = (mine + other[these, :]) / lengths[these, :]
    for b in range(blocks):
        swap(b).wait_send()
    send(last, me, 2, False)
    for c in range(last + 1):
        for hops in range(LINE):
            stage(c, hops, False)


def gathered(n, doc_grads, query_grads, doc_lengths):
    n_docs, layers, depth = doc_grads.shape
    rows = query_grads.shape[0]
    queries = rows * n
    cuts = pieces_of(depth)
    count = len(cuts)
    hbm = pl.BlockSpec(memory_space=pl.ANY)
    vmem = pl.BlockSpec(memory_space=pltpu.VMEM)
    return pl.pallas_call(
        functools.partial(kernel, cuts),
        out_shape=jax.ShapeDtypeStruct((n_docs, queries // 2), jnp.float32),
        in_specs=[hbm, hbm, vmem],
        out_specs=vmem,
        scratch_shapes=[
            pltpu.VMEM((n_docs, layers, depth), jnp.bfloat16),
            pltpu.VMEM((rows, layers, depth), jnp.bfloat16),
            pltpu.VMEM((layers, queries, depth), jnp.bfloat16),
            pltpu.VMEM((n_docs, queries), jnp.float32),
            pltpu.VMEM((n_docs, queries // 2), jnp.float32),
            pltpu.VMEM((n_docs, 128), jnp.float32),
            pltpu.SemaphoreType.DMA((count,)),
            pltpu.SemaphoreType.DMA((count,)),
            pltpu.SemaphoreType.DMA((3, count, n)),
            pltpu.SemaphoreType.DMA((count, n)),
            pltpu.SemaphoreType.DMA((3,)),
            pltpu.SemaphoreType.DMA((3,)),
        ],
        compiler_params=pltpu.CompilerParams(
            collective_id=0, has_side_effects=True, vmem_limit_bytes=58 * 2**20
        ),
        cost_estimate=pl.CostEstimate(
            flops=2 * n_docs * queries * layers * depth,
            bytes_accessed=2 * (n_docs + rows) * layers * depth,
            transcendentals=0,
        ),
    )(doc_grads, query_grads, doc_lengths.reshape(n_docs // 128, 128))


def plain(doc_grads, query_grads, doc_lengths):
    partial_value = jnp.einsum(
        "dlp,qlp->dq",
        doc_grads,
        lax.all_gather(query_grads, "docs", axis=0, tiled=True),
        preferred_element_type=jnp.float32,
    )
    summed = lax.psum_scatter(partial_value, "layers", scatter_dimension=1, tiled=True)
    return summed / doc_lengths.astype(jnp.float32)[:, None]


def solution(mesh):
    n = mesh.shape["docs"]

    def on_device(doc_grads, query_grads, doc_lengths):
        fits = (
            n == 2 * LINE
            and mesh.shape["layers"] == 2
            and doc_grads.shape[1] == 2
            and doc_grads.shape[0] % 384 == 0
            and doc_grads.shape[2] % 128 == 0
            and query_grads.shape[0] * n == 256
        )
        if fits:
            return gathered(n, doc_grads, query_grads, doc_lengths)
        return plain(doc_grads, query_grads, doc_lengths)

    in_specs = (
        P(("groups", "docs"), "layers", None),
        P(("groups", "docs"), "layers", None),
        P(("groups", "docs")),
    )
    out_specs = P(("groups", "docs"), "layers")
    return jax.shard_map(
        on_device, mesh=mesh, in_specs=in_specs, out_specs=out_specs, check_vma=False
    )
```

```python
import functools

import jax
import jax.numpy as jnp
from jax import lax
from jax.experimental import pallas as pl
from jax.experimental.pallas import tpu as pltpu
from jax.sharding import PartitionSpec as P

LINE = 4
LAST = 640
STEP = 512
LAG = 6


def pieces_of(depth):
    cuts, at = [], 0
    while at < depth - LAST:
        size = min(STEP, depth - LAST - at)
        cuts.append((at, size))
        at += size
    return cuts + [(at, depth - at)]


def kernel(cuts, docs_ref, q_ref, len_ref, out_ref, docs, own_q, held, acc, other, lengths,
           doc_sem, q_sem, send_sem, recv_sem, x_send, x_recv):
    me = lax.axis_index("docs")
    core = lax.axis_index("layers")
    z, y = me // 2, me % 2
    across = z * 2 + (1 - y)
    rows = q_ref.shape[0]
    last = len(cuts) - 1
    n_docs = docs.shape[0]
    half = out_ref.shape[1]

    def q_copy(c):
        at, size = cuts[c]
        cols = pl.ds(at, size)
        return pltpu.make_async_copy(q_ref.at[:, :, cols], own_q.at[:, :, cols], q_sem.at[c])

    def doc_copy(c):
        at, size = cuts[c]
        cols = pl.ds(at, size)
        return pltpu.make_async_copy(docs_ref.at[:, :, cols], docs.at[:, :, cols], doc_sem.at[c])

    first = [0, last] + list(range(1, last))
    for c in first:
        q_copy(c).start()
    for c in range(last + 1):
        doc_copy(c).start()

    barrier = pltpu.get_barrier_semaphore()

    def greet(target):
        pl.semaphore_signal(barrier, inc=1, device_id=target, device_id_type=pl.DeviceIdType.MESH)

    greet({"docs": across})
    greet({"layers": 1 - core})

    @pl.when(z < LINE - 1)
    def _():
        greet({"docs": me + 2})

    @pl.when(z > 0)
    def _():
        greet({"docs": me - 2})

    def take_own(c):
        at, size = cuts[c]
        q_copy(c).wait()
        mine = pl.ds(pl.multiple_of(me * rows, rows), rows)
        for layer in range(2):
            held[layer, mine, pl.ds(at, size)] = own_q[:, layer, pl.ds(at, size)]

    take_own(0)
    take_own(last)

    pl.semaphore_wait(barrier, 2 + (z + LINE - 1) // LINE + (2 * LINE - 2 - z) // LINE)

    def copy(c, src, way):
        at, size = cuts[c]
        block = held.at[:, pl.ds(pl.multiple_of(src * rows, rows), rows), pl.ds(at, size)]
        return pltpu.make_async_remote_copy(
            src_ref=block,
            dst_ref=block,
            send_sem=send_sem.at[way, c, src],
            recv_sem=recv_sem.at[c, src],
            device_id={"docs": (me + 2, me - 2, across)[way]},
            device_id_type=pl.DeviceIdType.MESH,
        )

    def arrived(c, src, start):
        if start:
            copy(c, src, 2).wait_recv()

    def send(c, src, way, start):
        def act():
            if start:
                copy(c, src, way).start()
            else:
                copy(c, src, way).wait_send()

        if way == 0:
            pl.when(z < LINE - 1)(act)
        elif way == 1:
            pl.when(z > 0)(act)
        else:
            act()

    def stage(c, hops, start=True):
        if hops == 0:
            send(c, me, 0, start)
            send(c, me, 1, start)
            if c == last:
                arrived(c, across, start)
                send(c, across, 0, start)
                send(c, across, 1, start)
            else:
                send(c, me, 2, start)
            return
        for lane in (y,) if c < last else (y, 1 - y):

            @pl.when(z >= hops)
            def _():
                src = (z - hops) * 2 + lane
                arrived(c, src, start)
                send(c, src, 0, start)
                if c < last:
                    send(c, src, 2, start)

            @pl.when(z + hops < LINE)
            def _():
                src = (z + hops) * 2 + lane
                arrived(c, src, start)
                send(c, src, 1, start)
                if c < last:
                    send(c, src, 2, start)

    def add(c, at_row, n_rows, first_one):
        at, size = cuts[c]
        these = pl.ds(at_row, n_rows)
        cols = pl.ds(at, size)
        total = None
        for layer in range(2):
            term = lax.dot_general(
                docs[these, layer, cols], held[layer, :, cols], (((1,), (1,)), ((), ())),
                preferred_element_type=jnp.float32,
            )
            total = term if total is None else total + term
        if first_one:
            acc[these, :] = total
        else:
            acc[these, :] += total

    def compute(c):
        doc_copy(c).wait()
        for line in range(LINE):
            arrived(c, line * 2 + (1 - y), True)
        add(c, 0, n_docs, c == 0)

    stage(0, 0)
    send(last, me, 2, True)
    for r in range(n_docs // 128):
        row = len_ref[pl.ds(r, 1), :].astype(jnp.float32)
        lengths[pl.ds(r * 128, 128), :] = jnp.broadcast_to(row, (128, 128)).T
    take_own(1)
    stage(1, 0)
    done = 0
    for step in range(1, last + LINE):
        if step + 1 < last:
            take_own(step + 1)
        if step + 1 <= last:
            stage(step + 1, 0)
        for hops in range(1, LINE):
            if 0 <= step - hops <= last:
                stage(step - hops, hops)
        if step >= LAG and done < last:
            compute(done)
            done += 1
    while done < last:
        compute(done)
        done += 1

    doc_copy(last).wait()
    blocks = 3
    height = n_docs // blocks

    def swap(b):
        these = pl.ds(b * height, height)
        return pltpu.make_async_remote_copy(
            src_ref=acc.at[these, pl.ds(pl.multiple_of((1 - core) * half, half), half)],
            dst_ref=other.at[these, :],
            send_sem=x_send.at[b],
            recv_sem=x_recv.at[b],
            device_id={"layers": 1 - core},
            device_id_type=pl.DeviceIdType.MESH,
        )

    for b in range(blocks):
        add(last, b * height, height, False)
        swap(b).start()
    for b in range(blocks):
        these = pl.ds(b * height, height)
        swap(b).wait_recv()
        mine = acc[these, pl.ds(pl.multiple_of(core * half, half), half)]
        out_ref[these, :] = (mine + other[these, :]) / lengths[these, :]
    for b in range(blocks):
        swap(b).wait_send()
    send(last, me, 2, False)
    for c in range(last + 1):
        for hops in range(LINE):
            stage(c, hops, False)


def gathered(n, doc_grads, query_grads, doc_lengths):
    n_docs, layers, depth = doc_grads.shape
    rows = query_grads.shape[0]
    queries = rows * n
    cuts = pieces_of(depth)
    count = len(cuts)
    hbm = pl.BlockSpec(memory_space=pl.ANY)
    vmem = pl.BlockSpec(memory_space=pltpu.VMEM)
    return pl.pallas_call(
        functools.partial(kernel, cuts),
        out_shape=jax.ShapeDtypeStruct((n_docs, queries // 2), jnp.float32),
        in_specs=[hbm, hbm, vmem],
        out_specs=vmem,
        scratch_shapes=[
            pltpu.VMEM((n_docs, layers, depth), jnp.bfloat16),
            pltpu.VMEM((rows, layers, depth), jnp.bfloat16),
            pltpu.VMEM((layers, queries, depth), jnp.bfloat16),
            pltpu.VMEM((n_docs, queries), jnp.float32),
            pltpu.VMEM((n_docs, queries // 2), jnp.float32),
            pltpu.VMEM((n_docs, 128), jnp.float32),
            pltpu.SemaphoreType.DMA((count,)),
            pltpu.SemaphoreType.DMA((count,)),
            pltpu.SemaphoreType.DMA((3, count, n)),
            pltpu.SemaphoreType.DMA((count, n)),
            pltpu.SemaphoreType.DMA((3,)),
            pltpu.SemaphoreType.DMA((3,)),
        ],
        compiler_params=pltpu.CompilerParams(
            collective_id=0, has_side_effects=True, vmem_limit_bytes=58 * 2**20
        ),
        cost_estimate=pl.CostEstimate(
            flops=2 * n_docs * queries * layers * depth,
            bytes_accessed=2 * (n_docs + rows) * layers * depth,
            transcendentals=0,
        ),
    )(doc_grads, query_grads, doc_lengths.reshape(n_docs // 128, 128))


def plain(doc_grads, query_grads, doc_lengths):
    partial_value = jnp.einsum(
        "dlp,qlp->dq",
        doc_grads,
        lax.all_gather(query_grads, "docs", axis=0, tiled=True),
        preferred_element_type=jnp.float32,
    )
    summed = lax.psum_scatter(partial_value, "layers", scatter_dimension=1, tiled=True)
    return summed / doc_lengths.astype(jnp.float32)[:, None]


def solution(mesh):
    n = mesh.shape["docs"]

    def on_device(doc_grads, query_grads, doc_lengths):
        fits = (
            n == 2 * LINE
            and mesh.shape["layers"] == 2
            and doc_grads.shape[1] == 2
            and doc_grads.shape[0] % 384 == 0
            and doc_grads.shape[2] % 128 == 0
            and query_grads.shape[0] * n == 256
        )
        if fits:
            return gathered(n, doc_grads, query_grads, doc_lengths)
        return plain(doc_grads, query_grads, doc_lengths)

    in_specs = (
        P(("groups", "docs"), "layers", None),
        P(("groups", "docs"), "layers", None),
        P(("groups", "docs")),
    )
    out_specs = P(("groups", "docs"), "layers")
    return jax.shard_map(
        on_device, mesh=mesh, in_specs=in_specs, out_specs=out_specs, check_vma=False
    )
```
